128 devices in a mesh: inst: 8 (over z_hi, x), slab: 16 (over z_lo, y, core).
Axes of the slice: x: 4, y: 4, z: 4 (z_hi: 2, z_lo: 2; z = z_hi * 2 + z_lo), core: 2. Of those that a mesh axis runs over, the one named last changes fastest.
Arguments:
- prior_disp: float32 [16, 3, 32, 128, 512], P('inst', None, 'slab'), may hold values from -6 to 6
- surface_disp: float32 [16, 3, 16384], P('inst', None, 'slab'), may hold values from -6 to 6
- springs: float32 [3, 32, 128, 512], P(None, 'slab'), may hold values from 0.2 to 5
- wall_row: int32 [32, 512], P('slab'), may hold values from 0 to 16383
- wall_mask: int32 [32, 512], P('slab'), may hold values 0 or 1
Outputs:
- displacement: float32 [16, 3, 32, 128, 512], P('inst', None, 'slab')
- grid_velocity: float32 [16, 3, 32, 128, 512], P('inst', None, 'slab')
The draws below stay inside these ranges and needn't reach their ends.
Inputs may be any that keep to these rules, and one draw needn't show every extreme that they name: `wall_row`: each wall cell names one structural surface node.
All inputs are finite; a program needn't handle non-finite values. No bound on the sum of `wall_mask` on one device may be relied on, other than what follows from the above.
Results may differ from the reference program's by a relative error of at most 0.000078.
Values sent between devices are 32-bit elements; how exact they have to be, the bound alone decides.
A program may use at most 128 MiB of HBM per device.

```python
import math
import jax
import jax.numpy as jnp
from jax import lax

NJ = 128
NK = 512
SWEEPS = 8
INSTANCES = 16
PLANES = 32
SURF = 16384


def plant(values, own_key, least, largest):
    index_at = [jax.random.randint(jax.random.fold_in(own_key, axis), (), 0, length) for axis, length in enumerate(values.shape)]
    longest = values.shape.index(max(values.shape))
    next_to = index_at[:longest] + [(index_at[longest] + 1) % values.shape[longest]] + index_at[longest + 1:]
    return values.at[tuple(index_at)].set(least).at[tuple(next_to)].set(largest)


def block_levels(rng, shape, pieces, low, high):
    factor_of = 1.0
    for position, blocks in pieces:
        steps = jax.random.uniform(jax.random.fold_in(jax.random.fold_in(rng, 6), position), (blocks,), jnp.float32, low / len(pieces), high / len(pieces))
        factor_of = factor_of * jnp.repeat(jnp.exp(steps), shape[position] // blocks).reshape((-1,) + (1,) * (len(shape) - 1 - position))
    return factor_of


def normal_values(stream_key, shape, scale, bound, pieces=(), held_as=jnp.bfloat16):
    values = scale * jax.random.normal(stream_key, shape, jnp.float32)
    if pieces:
        values = values * block_levels(stream_key, shape, pieces, -0.22, 0.18)
    return jnp.clip(values, -bound, bound).astype(held_as)


def setup_inputs(seed: int = 0) -> dict:
    keys = jax.random.split(jax.random.key(seed), 6)
    return {
        "prior_disp": normal_values(keys[0], (INSTANCES, 3, PLANES, NJ, NK), 1.0, 6.0, ((0, 8), (2, 16)), jnp.float32),
        "surface_disp": normal_values(keys[1], (INSTANCES, 3, SURF), 1.0, 6.0, ((0, 8), (2, 16)), jnp.float32),
        "springs": jnp.clip(jnp.exp(math.log(5.0) - 3.218876 * jax.random.uniform(keys[2], (3, PLANES, NJ, NK), jnp.float32) ** block_levels(keys[2], (3, PLANES, NJ, NK), ((1, 16),), -0.2, 0.2)), 0.2, 5.0),
        "wall_row": plant(jax.random.randint(keys[3], (PLANES, NK), 0, SURF), jax.random.fold_in(keys[3], 1), 0, SURF - 1).astype(jnp.int32),
        "wall_mask": plant((jax.random.randint(keys[4], (PLANES, NK), 0, 3) < 2).astype(jnp.int32), jax.random.fold_in(keys[4], 1), 0, 1),
    }


RELAXATION = 0.9


def relax_sweep(padded, springs, wall_disp, released):
    centre = padded[:, :, 1:-1]
    along_planes = padded[:, :, 2:] + padded[:, :, :-2]
    ghost_row = wall_disp + released * centre[:, :, :, 0, :]
    row_below = jnp.concatenate([ghost_row[:, :, :, None, :], centre[:, :, :, :-1, :]], axis=3)
    row_above = jnp.concatenate([centre[:, :, :, 1:, :], jnp.zeros_like(centre[:, :, :, :1, :])], axis=3)
    beside_all = jnp.roll(centre, 1, axis=4) + jnp.roll(centre, -1, axis=4)
    weighted = springs[0] * along_planes + springs[1] * (row_below + row_above) + springs[2] * beside_all
    weight = 2.0 * (springs[0] + springs[1] + springs[2])
    return centre + RELAXATION * (weighted / weight - centre)


def spectral(row_inst, col_inst, total_inst):
    offset = row_inst[:, None] - col_inst[None, :]
    parity = 1.0 - 2.0 * jnp.mod(offset, 2).astype(jnp.float32)
    phase_angle = jnp.pi * offset.astype(jnp.float32) / total_inst
    guarded = jnp.where(offset == 0, jnp.float32(0.5 * jnp.pi), phase_angle)
    entries = 0.5 * parity * jnp.cos(guarded) / jnp.sin(guarded)
    entries = jnp.where(offset == 0, jnp.float32(0.0), entries)
    return (2.0 * jnp.pi / total_inst) * entries


def reference(prior_disp, surface_disp, springs, wall_row, wall_mask):
    clamped = wall_mask.astype(jnp.float32)
    released = 1.0 - clamped

    def solve_instance(inputs_pair):
        start_disp, surface_rows = inputs_pair
        wall_disp = clamped * jnp.take(surface_rows, wall_row, axis=1)
        displaced = start_disp
        for sweep_index in range(SWEEPS):
            padded = jnp.pad(displaced, ((0, 0), (1, 1), (0, 0), (0, 0)))
            displaced = relax_sweep(padded[None], springs, wall_disp[None], released)[0]
        return displaced

    displacement = lax.map(solve_instance, (prior_disp, surface_disp))
    everyone = jnp.arange(INSTANCES, dtype=jnp.int32)
    matrix = spectral(everyone, everyone, INSTANCES)
    flat = displacement.reshape(INSTANCES, -1)
    grid_velocity = jnp.dot(matrix, flat, precision=lax.Precision.HIGHEST).reshape(displacement.shape)
    return displacement, grid_velocity
```

```python
import math

import jax
import jax.numpy as jnp
from jax import lax
from jax.experimental import pallas as pl
from jax.experimental.pallas import tpu as pltpu
from jax.sharding import PartitionSpec as P

MESH = pl.DeviceIdType.MESH
SWEEPS = 8
ROWS = 48
INSTANCES = 16
GROUP = 8
INST_DEVICES = 8
CORE_ROWS = 32
SHARE = 16
LANES = 512


def rate_factor(d):
    return 2.0 * math.pi / INSTANCES * 0.5 * (-1.0) ** d / math.tan(math.pi * d / INSTANCES)


def window_start(row_block):
    return pl.multiple_of(
        32 * row_block - 8 + 8 * ((3 - row_block) // 3) - 8 * (row_block // 3), 8
    )


def kernel(
    prior, surface, springs, code,
    disp_out, vel_out,
    field, coef, own_springs, own_coef, disp, vel_in, rate, table, codes, wall, free,
    in_send, in_recv, coef_send, coef_recv, table_send, table_recv, code_send, code_recv,
    edge_send, edge_recv, out_send, out_recv, vin_send, vin_recv, vout_send, vout_recv,
    local_sem, disp_sem,
):
    inst = lax.axis_index("inst")
    slab = lax.axis_index("slab")
    half = slab // GROUP
    rank = slab % GROUP
    row_block = rank // 2
    core = rank % 2
    partner = (1 - half) * GROUP + rank
    edge = 16 - 15 * half
    step_dir = 2 * half - 1

    spring_load = pltpu.make_async_copy(springs, own_springs, local_sem.at[0])
    spring_load.start()

    barrier = pltpu.get_barrier_semaphore()
    for shift in range(1, 2 * GROUP):
        pl.semaphore_signal(
            barrier, inc=1, device_id=(inst, (slab + shift) % (2 * GROUP)), device_id_type=MESH
        )
    for shift in range(1, INST_DEVICES):
        pl.semaphore_signal(
            barrier, inc=1, device_id=((inst + shift) % INST_DEVICES, slab), device_id_type=MESH
        )
    pl.semaphore_wait(barrier, 2 * GROUP - 1 + INST_DEVICES - 1)

    def remote(src, dst, send, recv, device):
        return pltpu.make_async_remote_copy(
            src_ref=src, dst_ref=dst, send_sem=send, recv_sem=recv,
            device_id=device, device_id_type=MESH,
        )

    def wait_bytes(ref, sem):
        pltpu.make_async_copy(ref, ref, sem).wait()

    for to_half in range(2):
        for to_core in range(2):
            target = to_half * GROUP + to_core
            piece = table.at[:, pl.ds(pl.multiple_of(slab * 8, 8), 8), :]

            @pl.when(target != slab)
            def _():
                remote(surface.at[to_core], piece, table_send, table_recv, (inst, target)).start()

            @pl.when(target == slab)
            def _():
                pltpu.make_async_copy(surface.at[to_core], piece, table_recv).start()

    for to_core in range(2):
        target = half * GROUP + to_core

        @pl.when(target != slab)
        def _():
            remote(code, codes.at[rank], code_send, code_recv, (inst, target)).start()

        @pl.when(target == slab)
        def _():
            pltpu.make_async_copy(code, codes.at[rank], code_recv).start()

    def start_in(c):
        dst = field.at[0, c, pl.ds(1 + 2 * rank, 2)]
        pltpu.make_async_copy(
            prior.at[core, c, :, pl.ds(window_start(row_block), ROWS), :], dst, in_recv.at[c]
        ).start()
        for shift in range(1, GROUP):
            to = (rank + shift) % GROUP
            remote(
                prior.at[to % 2, c, :, pl.ds(window_start(to // 2), ROWS), :], dst,
                in_send.at[c], in_recv.at[c], (inst, half * GROUP + to),
            ).start()

    start_in(0)

    spring_load.wait()

    @pl.loop(0, 2)
    def _(p):
        @pl.loop(0, 16)
        def _(t):
            rows = pl.ds(pl.multiple_of(8 * t, 8), 8)
            s0 = own_springs[0, p, rows, :]
            s1 = own_springs[1, p, rows, :]
            s2 = own_springs[2, p, rows, :]
            scale = 0.45 / (s0 + s1 + s2)
            own_coef[0, p, rows, :] = s0 * scale
            own_coef[1, p, rows, :] = s1 * scale

    coef_dst = coef.at[:, pl.ds(2 * rank, 2)]
    pltpu.make_async_copy(
        own_coef.at[:, :, pl.ds(window_start(row_block), ROWS), :], coef_dst, coef_recv
    ).start()
    for shift in range(1, GROUP):
        to = (rank + shift) % GROUP
        remote(
            own_coef.at[:, :, pl.ds(window_start(to // 2), ROWS), :], coef_dst,
            coef_send, coef_recv, (inst, half * GROUP + to),
        ).start()

    start_in(1)
    start_in(2)

    zero = jnp.zeros((8, LANES), jnp.float32)

    @pl.loop(0, 6)
    def _(i):
        for t in range(ROWS // 8):
            field[i // 3, i % 3, 17 * half, 8 * t : 8 * t + 8, :] = zero

    @pl.loop(0, 16)
    def _(p):
        free[p] = zero
        for c in range(3):
            wall[c, p] = zero

    @pl.when(row_block == 0)
    def _():
        wait_bytes(table, table_recv)
        wait_bytes(codes, code_recv)
        low = [codes[s] & 127 for s in range(GROUP)]
        high = [codes[s] >> 7 for s in range(GROUP)]

        def pick(h, picked):
            hits = [high[s] == h for s in range(GROUP)]
            result = []
            for c in range(3):
                row = jnp.broadcast_to(table[c, pl.ds(h, 1), :], (8, 128))
                for s in range(GROUP):
                    value = jnp.take_along_axis(row, low[s], axis=1, mode="promise_in_bounds")
                    result.append(jnp.where(hits[s], value, picked[c * GROUP + s]))
            return tuple(result)

        picked = lax.fori_loop(
            0, 128, pick, tuple(jnp.zeros((8, 128), jnp.float32) for _ in range(3 * GROUP))
        )
        for s in range(GROUP):
            released = (codes[s] < 0).astype(jnp.float32)
            for row in range(8):
                lanes = slice(128 * (row % 4), 128 * (row % 4) + 128)
                free[2 * s + row // 4, 0:1, lanes] = released[row : row + 1, :]
                for c in range(3):
                    wall[c, 2 * s + row // 4, 0:1, lanes] = picked[c * GROUP + s][row : row + 1, :]

    row_index = lax.broadcasted_iota(jnp.int32, (8, LANES), 0)
    first = row_index == 0
    last = row_index == 7

    def relax_plane(c, now, later, p):
        tiles = ROWS // 8
        u = [field[now, c, p, 8 * t : 8 * t + 8, :] for t in range(tiles)]
        down = [pltpu.roll(v, 1, 0) for v in u]
        up = [pltpu.roll(v, 7, 0) for v in u]
        ghost = wall[c, p - 1, 0:1, :] + free[p - 1, 0:1, :] * u[0][0:1, :]
        for t in range(tiles):
            rows = slice(8 * t, 8 * t + 8)
            below = jnp.where(first, down[t - 1] if t else ghost, down[t])
            above = jnp.where(last, up[t + 1] if t + 1 < tiles else 0.0, up[t])
            beside = pltpu.roll(u[t], 1, 1) + pltpu.roll(u[t], LANES - 1, 1)
            planes = field[now, c, p - 1, rows, :] + field[now, c, p + 1, rows, :]
            field[later, c, p, rows, :] = (
                0.1 * u[t] + 0.45 * beside
                + coef[0, p - 1, rows, :] * (planes - beside)
                + coef[1, p - 1, rows, :] * ((below + above) - beside)
            )

    def edge_copy(c, slot):
        return remote(
            field.at[slot, c, edge], field.at[slot, c, 17 * half],
            edge_send.at[c, slot], edge_recv.at[c, slot], (inst, partner),
        )

    def sweep(c, s):
        now = s % 2
        later = 1 - now
        edge_copy(c, now).wait_recv()
        relax_plane(c, now, later, edge)

        @pl.when(s < SWEEPS - 1)
        def _():
            edge_copy(c, later).start()

        @pl.loop(1, 16)
        def _(i):
            relax_plane(c, now, later, edge + i * step_dir)

        edge_copy(c, now).wait_send()

    def begin_sweeps(c):
        wait_bytes(field.at[0, c, pl.ds(1, 16)], in_recv.at[c])
        edge_copy(c, 0).start()

    def sweeps(c, low, high):
        @pl.loop(low, high)
        def _(s):
            sweep(c, s)

    own_rows = pl.multiple_of(32 * row_block - window_start(row_block), 8)

    def start_out(c):
        dst = disp.at[core, c, :, pl.ds(pl.multiple_of(CORE_ROWS * row_block, 8), CORE_ROWS), :]
        pltpu.make_async_copy(
            field.at[0, c, pl.ds(1 + 2 * rank, 2), pl.ds(own_rows, CORE_ROWS), :],
            dst, out_recv.at[c],
        ).start()
        for shift in range(1, GROUP):
            to = (rank + shift) % GROUP
            remote(
                field.at[0, c, pl.ds(1 + 2 * to, 2), pl.ds(own_rows, CORE_ROWS), :], dst,
                out_send.at[c], out_recv.at[c], (inst, half * GROUP + to),
            ).start()

    def disp_copy(c):
        return pltpu.make_async_copy(disp.at[:, c], disp_out.at[:, c], disp_sem.at[c])

    def start_vin(c):
        wait_bytes(disp.at[:, c], out_recv.at[c])
        dst = vel_in.at[pl.ds(2 * inst, 2), c]
        for shift in range(1, INST_DEVICES):
            to = (inst + shift) % INST_DEVICES
            remote(
                disp.at[:, c, :, pl.ds(pl.multiple_of(SHARE * to, 8), SHARE), :], dst,
                vin_send.at[c], vin_recv.at[c], (to, slab),
            ).start()
        pltpu.make_async_copy(
            disp.at[:, c, :, pl.ds(pl.multiple_of(SHARE * inst, 8), SHARE), :], dst, vin_recv.at[c]
        ).start()
        disp_copy(c).start()

    def start_vout(c):
        wait_bytes(vel_in.at[:, c], vin_recv.at[c])

        @pl.loop(0, 4)
        def _(i):
            rows = pl.ds(pl.multiple_of(8 * (i % 2), 8), 8)
            for lane in range(0, LANES, 128):
                lanes = slice(lane, lane + 128)
                u = [vel_in[n, c, i // 2, rows, lanes] for n in range(INSTANCES)]
                for n in range(INSTANCES):
                    total = None
                    for d in range(1, 8):
                        term = rate_factor(d) * (u[(n - d) % INSTANCES] - u[(n + d) % INSTANCES])
                        total = term if total is None else total + term
                    rate[n, c, i // 2, rows, lanes] = total

        dst = vel_out.at[:, c, :, pl.ds(pl.multiple_of(SHARE * inst, 8), SHARE), :]
        for shift in range(1, INST_DEVICES):
            to = (inst + shift) % INST_DEVICES
            remote(
                rate.at[pl.ds(2 * to, 2), c], dst,
                vout_send.at[c], vout_recv.at[c], (to, slab),
            ).start()
        pltpu.make_async_copy(rate.at[pl.ds(2 * inst, 2), c], dst, vout_recv.at[c]).start()

    wait_bytes(coef, coef_recv)
    begin_sweeps(0)
    sweeps(0, 0, SWEEPS)
    start_out(0)
    begin_sweeps(1)
    sweeps(1, 0, 4)
    start_vin(0)
    sweeps(1, 4, SWEEPS)
    start_out(1)
    begin_sweeps(2)
    start_vout(0)
    sweeps(2, 0, 4)
    start_vin(1)
    sweeps(2, 4, SWEEPS)
    start_out(2)
    start_vout(1)
    start_vin(2)
    start_vout(2)

    for c in range(3):
        disp_copy(c).wait()
        wait_bytes(vel_out.at[:, c], vout_recv.at[c])
        wait_bytes(field.at[0, c, pl.ds(1, 14)], in_send.at[c])
        wait_bytes(field.at[0, c, pl.ds(1, 14), pl.ds(0, CORE_ROWS), :], out_send.at[c])
        wait_bytes(vel_in.at[pl.ds(0, 14), c], vin_send.at[c])
        wait_bytes(rate.at[pl.ds(0, 14), c], vout_send.at[c])
    wait_bytes(coef.at[:, pl.ds(0, 14)], coef_send)
    wait_bytes(table.at[:, pl.ds(0, 24)], table_send)
    wait_bytes(codes.at[0], code_send)

    @pl.when(row_block != 0)
    def _():
        wait_bytes(table.at[:, pl.ds(0, 8)], table_send)
        wait_bytes(codes.at[0], code_send)


def per_device(prior_disp, surface_disp, springs, wall_row, wall_mask):
    surface = surface_disp.reshape(2, 3, 8, 128)
    code = jnp.where(wall_mask != 0, wall_row, -1).reshape(8, 128)
    f32 = jnp.float32
    dma = pltpu.SemaphoreType.DMA
    shape = jax.ShapeDtypeStruct(prior_disp.shape, f32)
    return pl.pallas_call(
        kernel,
        out_shape=(shape, shape),
        in_specs=[pl.BlockSpec(memory_space=pl.ANY)] * 4,
        out_specs=(pl.BlockSpec(memory_space=pl.ANY),) * 2,
        scratch_shapes=[
            pltpu.VMEM((2, 3, 18, ROWS, LANES), f32),
            pltpu.VMEM((2, 16, ROWS, LANES), f32),
            pltpu.VMEM((3, 2, 128, LANES), f32),
            pltpu.VMEM((2, 2, 128, LANES), f32),
            pltpu.VMEM((2, 3, 2, 128, LANES), f32),
            pltpu.VMEM((INSTANCES, 3, 2, SHARE, LANES), f32),
            pltpu.VMEM((INSTANCES, 3, 2, SHARE, LANES), f32),
            pltpu.VMEM((3, 128, 128), f32),
            pltpu.VMEM((GROUP, 8, 128), jnp.int32),
            pltpu.VMEM((3, 16, 8, LANES), f32),
            pltpu.VMEM((16, 8, LANES), f32),
            dma((3,)), dma((3,)), dma, dma, dma, dma, dma, dma,
            dma((3, 2)), dma((3, 2)), dma((3,)), dma((3,)), dma((3,)), dma((3,)),
            dma((3,)), dma((3,)),
            dma((1,)), dma((3,)),
        ],
        compiler_params=pltpu.CompilerParams(
            collective_id=0, has_side_effects=True, vmem_limit_bytes=48 * 1024 * 1024
        ),
    )(prior_disp, surface, springs, code)


def solution(mesh):
    in_specs = (
        P("inst", None, "slab", None, None),
        P("inst", None, "slab"),
        P(None, "slab", None, None),
        P("slab", None),
        P("slab", None),
    )
    out_specs = (P("inst", None, "slab", None, None), P("inst", None, "slab", None, None))
    return jax.shard_map(
        per_device, mesh=mesh, in_specs=in_specs, out_specs=out_specs, check_vma=False
    )
```

```python
import math

import jax
import jax.numpy as jnp
from jax import lax
from jax.experimental import pallas as pl
from jax.experimental.pallas import tpu as pltpu
from jax.sharding import PartitionSpec as P

MESH = pl.DeviceIdType.MESH
SWEEPS = 8
ROWS = 72
CORE_PLANES = 8
INSTANCES = 16
GROUP = 8
INST_DEVICES = 8
CORE_ROWS = 64
PIECES = 3
PIECE_ROWS = 24
DIRECT = 24
SHARE = 16
LANES = 512


def rate_factor(d):
    return 2.0 * math.pi / INSTANCES * 0.5 * (-1.0) ** d / math.tan(math.pi * d / INSTANCES)


INST_ORDER = (1, 3, 4, 7, 2, 5, 6)


def window(row_block, first=0, count=ROWS):
    return pl.ds(pl.multiple_of(56 * (row_block % 2) + first, 8), count)


def inst_partner(inst, offset):
    return (inst // 4 + offset // 4) % 2 * 4 + (inst + offset) % 4


def kernel(
    prior, surface, springs, code,
    disp, vel_out,
    field, coef, own_coef, vel_in, rate, table, codes, wall, free,
    in_send, in_recv, coef_send, coef_recv, part_send, part_recv, share_send, share_recv, table_send, table_recv, code_send, code_recv,
    edge_send, edge_recv, out_send, out_recv, vin_send, vin_recv, vout_send, vout_recv,
):
    inst = lax.axis_index("inst")
    slab = lax.axis_index("slab")
    half = slab // GROUP
    rank = slab % GROUP
    row_block = rank // 2
    core = rank % 2
    own_inst = row_block // 2
    chain = 2 * half + core

    barrier = pltpu.get_barrier_semaphore()
    for shift in range(1, 2 * GROUP):
        pl.semaphore_signal(
            barrier, inc=1, device_id=(inst, (slab + shift) % (2 * GROUP)), device_id_type=MESH
        )
    for shift in range(1, INST_DEVICES):
        pl.semaphore_signal(
            barrier, inc=1, device_id=((inst + shift) % INST_DEVICES, slab), device_id_type=MESH
        )
    pl.semaphore_wait(barrier, 2 * GROUP - 1 + INST_DEVICES - 1)

    def remote(src, dst, send, recv, device):
        return pltpu.make_async_remote_copy(
            src_ref=src, dst_ref=dst, send_sem=send, recv_sem=recv,
            device_id=device, device_id_type=MESH,
        )

    def wait_bytes(ref, sem):
        pltpu.make_async_copy(ref, ref, sem).wait()

    def table_sends(action):
        for n in range(2):
            for k in range(4):
                target = k // 2 * GROUP + 4 * n + k % 2
                action(surface.at[n], table.at[:, pl.ds(pl.multiple_of(slab * 8, 8), 8), :],
                       table_send, table_recv, target)

    def code_sends(action):
        for n in range(2):
            action(code, codes.at[rank % 4], code_send, code_recv,
                   half * GROUP + 4 * n + row_block // 2)

    def start_either(src, dst, send, recv, target):
        @pl.when(target != slab)
        def _():
            remote(src, dst, send, recv, (inst, target)).start()

        @pl.when(target == slab)
        def _():
            pltpu.make_async_copy(src, dst, recv).start()

    def finish_either(src, dst, send, recv, target):
        @pl.when(target != slab)
        def _():
            remote(src, dst, send, recv, (inst, target)).wait_send()

    def row_sends(action, source, dst, send, recv):
        for shift in (0, 1, 3, 2):
            to = (row_block + shift) % 4
            action(source(to), dst, send, recv, half * GROUP + 2 * to + row_block // 2)

    def in_sends(action, c):
        row_sends(action, lambda to: prior.at[to // 2, c, :, window(to), :],
                  field.at[0, c, pl.ds(1 + 2 * (rank % 4), 2)], in_send.at[c], in_recv.at[c])

    quarter = inst % 4
    shared = pl.ds(DIRECT, ROWS - DIRECT)

    def coef_sends(action):
        row_sends(action, lambda to: own_coef.at[:, window(to, 0, DIRECT), :],
                  coef.at[:, rank % 4, pl.ds(0, DIRECT)], coef_send, coef_recv)

    def part_sends(action):
        row_sends(action, lambda to: own_coef.at[quarter, window(to, DIRECT, ROWS - DIRECT), :],
                  coef.at[quarter, rank % 4, shared], part_send, part_recv)

    def start_in(c):
        in_sends(start_either, c)

    @pl.loop(0, 32)
    def _(i):
        p = i // 16
        rows = pl.ds(pl.multiple_of(8 * (i % 16), 8), 8)
        s0 = springs[0, p, rows, :]
        s1 = springs[1, p, rows, :]
        s2 = springs[2, p, rows, :]
        scale = 0.45 / (s0 + s1 + s2)
        own_coef[p, rows, :] = s0 * scale
        own_coef[2 + p, rows, :] = s1 * scale

    part_sends(start_either)
    table_sends(start_either)
    code_sends(start_either)
    start_in(0)
    coef_sends(start_either)

    wait_bytes(coef.at[0, :, shared], part_recv)
    for offset in (1, 3, 2):
        mine = coef.at[quarter, :, shared]
        remote(
            mine, mine, share_send, share_recv, (inst // 4 * 4 + (inst + offset) % 4, slab)
        ).start()

    zero = jnp.zeros((8, LANES), jnp.float32)

    @pl.loop(0, 6)
    def _(i):
        for t in range(ROWS // 8):
            rows = slice(8 * t, 8 * t + 8)

            @pl.when(chain == 0)
            def _():
                field[i // 3, i % 3, 0, rows, :] = zero

            @pl.when(chain == 3)
            def _():
                field[i // 3, i % 3, CORE_PLANES + 1, rows, :] = zero

    @pl.loop(0, CORE_PLANES)
    def _(p):
        free[p] = zero
        for c in range(3):
            wall[c, p] = zero

    @pl.when(row_block % 2 == 0)
    def _():
        wait_bytes(table, table_recv)
        wait_bytes(codes, code_recv)
        low = [codes[s] & 127 for s in range(4)]
        high = [codes[s] >> 7 for s in range(4)]

        def pick(h, picked):
            hits = [high[s] == h for s in range(4)]
            result = []
            for c in range(3):
                row = jnp.broadcast_to(table[c, pl.ds(h, 1), :], (8, 128))
                for s in range(4):
                    value = jnp.take_along_axis(row, low[s], axis=1, mode="promise_in_bounds")
                    result.append(jnp.where(hits[s], value, picked[c * 4 + s]))
            return tuple(result)

        picked = lax.fori_loop(
            0, 128, pick, tuple(jnp.zeros((8, 128), jnp.float32) for _ in range(12))
        )
        for s in range(4):
            released = (codes[s] < 0).astype(jnp.float32)
            for row in range(8):
                lanes = slice(128 * (row % 4), 128 * (row % 4) + 128)
                free[2 * s + row // 4, 0:1, lanes] = released[row : row + 1, :]
                for c in range(3):
                    wall[c, 2 * s + row // 4, 0:1, lanes] = picked[c * 4 + s][row : row + 1, :]

    row_index = lax.broadcasted_iota(jnp.int32, (8, LANES), 0)
    first = row_index == 0
    last = row_index == 7

    def relax_plane(c, now, later, p, piece=None):
        tiles = ROWS // 8
        per = PIECE_ROWS // 8
        wanted = range(tiles) if piece is None else range(piece * per, piece * per + per)
        near = range(max(wanted[0] - 1, 0), min(wanted[-1] + 2, tiles))
        u = {t: field[now, c, p, 8 * t : 8 * t + 8, :] for t in near}
        down = {t: pltpu.roll(u[t], 1, 0) for t in near}
        up = {t: pltpu.roll(u[t], 7, 0) for t in near}
        if 0 in u:
            ghost = wall[c, p - 1, 0:1, :] + free[p - 1, 0:1, :] * u[0][0:1, :]
        for t in wanted:
            rows = slice(8 * t, 8 * t + 8)
            below = jnp.where(first, down[t - 1] if t else ghost, down[t])
            above = jnp.where(last, up[t + 1] if t + 1 < tiles else 0.0, up[t])
            beside = pltpu.roll(u[t], 1, 1) + pltpu.roll(u[t], LANES - 1, 1)
            planes = field[now, c, p - 1, rows, :] + field[now, c, p + 1, rows, :]
            field[later, c, p, rows, :] = (
                0.1 * u[t] + 0.45 * beside
                + coef[(p - 1) % 2, (p - 1) // 2, rows, :] * (planes - beside)
                + coef[2 + (p - 1) % 2, (p - 1) // 2, rows, :] * ((below + above) - beside)
            )

    def piece_rows(piece):
        return pl.ds(piece * PIECE_ROWS, PIECE_ROWS)

    def edge_copy(c, now, upper, piece):
        to = (chain + (1 if upper else 3)) % 4
        target = to // 2 * GROUP + 2 * row_block + to % 2
        src, dst = (CORE_PLANES, 0) if upper else (1, CORE_PLANES + 1)
        return remote(
            field.at[now, c, src, piece_rows(piece)], field.at[now, c, dst, piece_rows(piece)],
            edge_send.at[c, now, upper, piece], edge_recv.at[c, now, 1 - upper, piece],
            (inst, target),
        )

    has = (chain > 0, chain < 3)

    def sweep(c, s):
        now = s % 2
        later = 1 - now
        for piece in range(PIECES):
            for upper in range(2):
                @pl.when(has[upper])
                def _():
                    wait_bytes(
                        field.at[now, c, 0, piece_rows(piece)], edge_recv.at[c, now, upper, piece]
                    )

                relax_plane(c, now, later, CORE_PLANES if upper else 1, piece)

                @pl.when(has[upper] & (s < SWEEPS - 1))
                def _():
                    edge_copy(c, later, upper, piece).start()

        @pl.loop(2, CORE_PLANES)
        def _(p):
            relax_plane(c, now, later, p)

        for upper in range(2):
            @pl.when(has[upper])
            def _():
                for piece in range(PIECES):
                    edge_copy(c, now, upper, piece).wait_send()

    def begin_sweeps(c):
        wait_bytes(field.at[0, c, pl.ds(1, CORE_PLANES)], in_recv.at[c])
        for upper in range(2):
            @pl.when(has[upper])
            def _():
                for piece in range(PIECES):
                    edge_copy(c, 0, upper, piece).start()

    def sweeps(count, *parts):
        @pl.loop(0, count)
        def _(s):
            for c, first_sweep in parts:
                sweep(c, first_sweep + s)

    def out_sends(action, c):
        own_rows = pl.ds(pl.multiple_of(8 * (row_block % 2), 8), CORE_ROWS)
        dst = disp.at[
            own_inst, c, :, pl.ds(pl.multiple_of(CORE_ROWS * (row_block % 2), 8), CORE_ROWS), :
        ]
        for shift in range(4):
            to = (rank + shift) % 4
            action(
                field.at[0, c, pl.ds(1 + 2 * to, 2), own_rows, :], dst,
                out_send.at[c], out_recv.at[c], half * GROUP + 4 * core + to,
            )

    def start_out(c):
        out_sends(start_either, c)

    def start_vin(c):
        wait_bytes(disp.at[:, c], out_recv.at[c])
        dst = vel_in.at[pl.ds(2 * inst, 2), c]
        for offset in INST_ORDER:
            to = inst_partner(inst, offset)
            remote(
                disp.at[:, c, :, pl.ds(pl.multiple_of(SHARE * to, 8), SHARE), :], dst,
                vin_send.at[c], vin_recv.at[c], (to, slab),
            ).start()
        pltpu.make_async_copy(
            disp.at[:, c, :, pl.ds(pl.multiple_of(SHARE * inst, 8), SHARE), :], dst, vin_recv.at[c]
        ).start()

    def start_vout(c):
        wait_bytes(vel_in.at[:, c], vin_recv.at[c])

        @pl.loop(0, 4)
        def _(i):
            rows = pl.ds(pl.multiple_of(8 * (i % 2), 8), 8)
            for lane in range(0, LANES, 128):
                lanes = slice(lane, lane + 128)
                u = [vel_in[n, c, i // 2, rows, lanes] for n in range(INSTANCES)]
                for n in range(INSTANCES):
                    total = None
                    for d in range(1, 8):
                        term = rate_factor(d) * (u[(n - d) % INSTANCES] - u[(n + d) % INSTANCES])
                        total = term if total is None else total + term
                    rate[n, c, i // 2, rows, lanes] = total

        dst = vel_out.at[:, c, :, pl.ds(pl.multiple_of(SHARE * inst, 8), SHARE), :]
        for offset in INST_ORDER:
            to = inst_partner(inst, offset)
            remote(
                rate.at[pl.ds(2 * to, 2), c], dst,
                vout_send.at[c], vout_recv.at[c], (to, slab),
            ).start()
        pltpu.make_async_copy(rate.at[pl.ds(2 * inst, 2), c], dst, vout_recv.at[c]).start()

    wait_bytes(coef.at[:, :, pl.ds(0, DIRECT)], coef_recv)
    wait_bytes(coef.at[pl.ds(0, 3), :, shared], share_recv)
    begin_sweeps(0)
    start_in(1)
    sweeps(4, (0, 0))
    begin_sweeps(1)
    start_in(2)
    sweeps(4, (0, 4), (1, 0))
    start_out(0)
    begin_sweeps(2)
    sweeps(2, (1, 4), (2, 0))
    start_vin(0)
    sweeps(2, (1, 6), (2, 2))
    start_out(1)
    sweeps(4, (2, 4))
    start_out(2)
    start_vin(1)
    start_vout(0)
    start_vin(2)
    start_vout(1)
    start_vout(2)

    for c in range(3):
        wait_bytes(vel_out.at[:, c], vout_recv.at[c])
        in_sends(finish_either, c)
        out_sends(finish_either, c)
        wait_bytes(vel_in.at[pl.ds(0, 14), c], vin_send.at[c])
        wait_bytes(rate.at[pl.ds(0, 14), c], vout_send.at[c])
    wait_bytes(coef.at[pl.ds(0, 3), :, shared], share_send)
    coef_sends(finish_either)
    part_sends(finish_either)
    table_sends(finish_either)
    code_sends(finish_either)


def per_device(prior_disp, surface_disp, springs, wall_row, wall_mask):
    surface = surface_disp.reshape(2, 3, 8, 128)
    code = jnp.where(wall_mask != 0, wall_row, -1).reshape(8, 128)
    f32 = jnp.float32
    dma = pltpu.SemaphoreType.DMA
    shape = jax.ShapeDtypeStruct(prior_disp.shape, f32)
    return pl.pallas_call(
        kernel,
        out_shape=(shape, shape),
        in_specs=[
            pl.BlockSpec(memory_space=pl.ANY),
            pl.BlockSpec(memory_space=pl.ANY),
            pl.BlockSpec(memory_space=pltpu.VMEM),
            pl.BlockSpec(memory_space=pl.ANY),
        ],
        out_specs=(pl.BlockSpec(memory_space=pltpu.VMEM),) * 2,
        scratch_shapes=[
            pltpu.VMEM((2, 3, CORE_PLANES + 2, ROWS, LANES), f32),
            pltpu.VMEM((4, CORE_PLANES // 2, ROWS, LANES), f32),
            pltpu.VMEM((4, 128, LANES), f32),
            pltpu.VMEM((INSTANCES, 3, 2, SHARE, LANES), f32),
            pltpu.VMEM((INSTANCES, 3, 2, SHARE, LANES), f32),
            pltpu.VMEM((3, 128, 128), f32),
            pltpu.VMEM((4, 8, 128), jnp.int32),
            pltpu.VMEM((3, CORE_PLANES, 8, LANES), f32),
            pltpu.VMEM((CORE_PLANES, 8, LANES), f32),
            dma((3,)), dma((3,)), dma, dma, dma, dma, dma, dma, dma, dma, dma, dma,
            dma((3, 2, 2, PIECES)), dma((3, 2, 2, PIECES)), dma((3,)), dma((3,)), dma((3,)), dma((3,)),
            dma((3,)), dma((3,)),
        ],
        compiler_params=pltpu.CompilerParams(
            collective_id=0, has_side_effects=True, vmem_limit_bytes=48 * 1024 * 1024
        ),
    )(prior_disp, surface, springs, code)


def solution(mesh):
    in_specs = (
        P("inst", None, "slab", None, None),
        P("inst", None, "slab"),
        P(None, "slab", None, None),
        P("slab", None),
        P("slab", None),
    )
    out_specs = (P("inst", None, "slab", None, None), P("inst", None, "slab", None, None))
    return jax.shard_map(
        per_device, mesh=mesh, in_specs=in_specs, out_specs=out_specs, check_vma=False
    )
```

```python
import math

import jax
import jax.numpy as jnp
from jax import lax
from jax.experimental import pallas as pl
from jax.experimental.pallas import tpu as pltpu
from jax.sharding import PartitionSpec as P

MESH = pl.DeviceIdType.MESH
SWEEPS = 8
ROWS = 72
CORE_PLANES = 8
INSTANCES = 16
GROUP = 8
INST_DEVICES = 8
CORE_ROWS = 64
PIECES = 3
PIECE_ROWS = 24
DIRECT = 16
SHARE = 16
LANES = 512


def rate_factor(d):
    return 2.0 * math.pi / INSTANCES * 0.5 * (-1.0) ** d / math.tan(math.pi * d / INSTANCES)


INST_ORDER = (1, 3, 4, 7, 2, 5, 6)


def window(row_block, first=0, count=ROWS):
    return pl.ds(pl.multiple_of(56 * (row_block % 2) + first, 8), count)


def inst_partner(inst, offset):
    return (inst // 4 + offset // 4) % 2 * 4 + (inst + offset) % 4


def kernel(
    prior, surface, springs, code,
    disp, vel_out,
    field, coef, own_coef, vel_in, rate, table, codes, wall, free,
    in_send, in_recv, coef_send, coef_recv, part_send, part_recv, share_send, share_recv, table_send, table_recv, code_send, code_recv,
    edge_send, edge_recv, out_send, out_recv, vin_send, vin_recv, vout_send, vout_recv,
):
    inst = lax.axis_index("inst")
    slab = lax.axis_index("slab")
    half = slab // GROUP
    rank = slab % GROUP
    row_block = rank // 2
    core = rank % 2
    own_inst = row_block // 2
    chain = 2 * half + core

    barrier = pltpu.get_barrier_semaphore()
    for shift in range(1, 2 * GROUP):
        pl.semaphore_signal(
            barrier, inc=1, device_id=(inst, (slab + shift) % (2 * GROUP)), device_id_type=MESH
        )
    for shift in range(1, INST_DEVICES):
        pl.semaphore_signal(
            barrier, inc=1, device_id=((inst + shift) % INST_DEVICES, slab), device_id_type=MESH
        )
    pl.semaphore_wait(barrier, 2 * GROUP - 1 + INST_DEVICES - 1)

    def remote(src, dst, send, recv, device):
        return pltpu.make_async_remote_copy(
            src_ref=src, dst_ref=dst, send_sem=send, recv_sem=recv,
            device_id=device, device_id_type=MESH,
        )

    def wait_bytes(ref, sem):
        pltpu.make_async_copy(ref, ref, sem).wait()

    def table_sends(action):
        for n in range(2):
            for k in range(4):
                target = k // 2 * GROUP + 4 * n + k % 2
                action(surface.at[n], table.at[:, pl.ds(pl.multiple_of(slab * 8, 8), 8), :],
                       table_send, table_recv, target)

    def code_sends(action):
        for n in range(2):
            action(code, codes.at[rank % 4], code_send, code_recv,
                   half * GROUP + 4 * n + row_block // 2)

    def start_either(src, dst, send, recv, target):
        @pl.when(target != slab)
        def _():
            remote(src, dst, send, recv, (inst, target)).start()

        @pl.when(target == slab)
        def _():
            pltpu.make_async_copy(src, dst, recv).start()

    def finish_either(src, dst, send, recv, target):
        @pl.when(target != slab)
        def _():
            remote(src, dst, send, recv, (inst, target)).wait_send()

    def row_sends(action, source, dst, send, recv):
        for shift in (0, 1, 3, 2):
            to = (row_block + shift) % 4
            action(source(to), dst, send, recv, half * GROUP + 2 * to + row_block // 2)

    def in_sends(action, c):
        row_sends(action, lambda to: prior.at[to // 2, c, :, window(to), :],
                  field.at[0, c, pl.ds(1 + 2 * (rank % 4), 2)], in_send.at[c], in_recv.at[c])

    quarter = inst % 4
    shared = pl.ds(DIRECT, ROWS - DIRECT)

    def coef_sends(action):
        row_sends(action, lambda to: own_coef.at[:, window(to, 0, DIRECT), :],
                  coef.at[:, rank % 4, pl.ds(0, DIRECT)], coef_send, coef_recv)

    def part_sends(action):
        row_sends(action, lambda to: own_coef.at[quarter, window(to, DIRECT, ROWS - DIRECT), :],
                  coef.at[quarter, rank % 4, shared], part_send, part_recv)

    def start_in(c):
        in_sends(start_either, c)

    @pl.loop(0, 32)
    def _(i):
        p = i // 16
        rows = pl.ds(pl.multiple_of(8 * (i % 16), 8), 8)
        s0 = springs[0, p, rows, :]
        s1 = springs[1, p, rows, :]
        s2 = springs[2, p, rows, :]
        scale = 0.45 / (s0 + s1 + s2)
        own_coef[p, rows, :] = s0 * scale
        own_coef[2 + p, rows, :] = s1 * scale

    part_sends(start_either)
    table_sends(start_either)
    code_sends(start_either)
    start_in(0)
    coef_sends(start_either)

    wait_bytes(coef.at[0, :, shared], part_recv)
    for offset in (1, 3, 2):
        mine = coef.at[quarter, :, shared]
        remote(
            mine, mine, share_send, share_recv, (inst // 4 * 4 + (inst + offset) % 4, slab)
        ).start()

    zero = jnp.zeros((8, LANES), jnp.float32)

    @pl.loop(0, 6)
    def _(i):
        for t in range(ROWS // 8):
            rows = slice(8 * t, 8 * t + 8)

            @pl.when(chain == 0)
            def _():
                field[i // 3, i % 3, 0, rows, :] = zero

            @pl.when(chain == 3)
            def _():
                field[i // 3, i % 3, CORE_PLANES + 1, rows, :] = zero

    @pl.loop(0, CORE_PLANES)
    def _(p):
        free[p] = zero
        for c in range(3):
            wall[c, p] = zero

    @pl.when(row_block % 2 == 0)
    def _():
        wait_bytes(table, table_recv)
        wait_bytes(codes, code_recv)
        low = [codes[s] & 127 for s in range(4)]
        high = [codes[s] >> 7 for s in range(4)]

        def pick(h, picked):
            hits = [high[s] == h for s in range(4)]
            result = []
            for c in range(3):
                row = jnp.broadcast_to(table[c, pl.ds(h, 1), :], (8, 128))
                for s in range(4):
                    value = jnp.take_along_axis(row, low[s], axis=1, mode="promise_in_bounds")
                    result.append(jnp.where(hits[s], value, picked[c * 4 + s]))
            return tuple(result)

        picked = lax.fori_loop(
            0, 128, pick, tuple(jnp.zeros((8, 128), jnp.float32) for _ in range(12))
        )
        for s in range(4):
            released = (codes[s] < 0).astype(jnp.float32)
            for row in range(8):
                lanes = slice(128 * (row % 4), 128 * (row % 4) + 128)
                free[2 * s + row // 4, 0:1, lanes] = released[row : row + 1, :]
                for c in range(3):
                    wall[c, 2 * s + row // 4, 0:1, lanes] = picked[c * 4 + s][row : row + 1, :]

    row_index = lax.broadcasted_iota(jnp.int32, (8, LANES), 0)
    first = row_index == 0
    last = row_index == 7

    def relax_plane(c, now, later, p, piece=None):
        tiles = ROWS // 8
        per = PIECE_ROWS // 8
        wanted = range(tiles) if piece is None else range(piece * per, piece * per + per)
        near = range(max(wanted[0] - 1, 0), min(wanted[-1] + 2, tiles))
        u = {t: field[now, c, p, 8 * t : 8 * t + 8, :] for t in near}
        down = {t: pltpu.roll(u[t], 1, 0) for t in near}
        up = {t: pltpu.roll(u[t], 7, 0) for t in near}
        if 0 in u:
            ghost = wall[c, p - 1, 0:1, :] + free[p - 1, 0:1, :] * u[0][0:1, :]
        for t in wanted:
            rows = slice(8 * t, 8 * t + 8)
            below = jnp.where(first, down[t - 1] if t else ghost, down[t])
            above = jnp.where(last, up[t + 1] if t + 1 < tiles else 0.0, up[t])
            beside = pltpu.roll(u[t], 1, 1) + pltpu.roll(u[t], LANES - 1, 1)
            planes = field[now, c, p - 1, rows, :] + field[now, c, p + 1, rows, :]
            field[later, c, p, rows, :] = (
                0.1 * u[t] + 0.45 * beside
                + coef[(p - 1) % 2, (p - 1) // 2, rows, :] * (planes - beside)
                + coef[2 + (p - 1) % 2, (p - 1) // 2, rows, :] * ((below + above) - beside)
            )

    def piece_rows(piece):
        return pl.ds(piece * PIECE_ROWS, PIECE_ROWS)

    def edge_copy(c, now, upper, piece):
        to = (chain + (1 if upper else 3)) % 4
        target = to // 2 * GROUP + 2 * row_block + to % 2
        src, dst = (CORE_PLANES, 0) if upper else (1, CORE_PLANES + 1)
        return remote(
            field.at[now, c, src, piece_rows(piece)], field.at[now, c, dst, piece_rows(piece)],
            edge_send.at[c, now, upper, piece], edge_recv.at[c, now, 1 - upper, piece],
            (inst, target),
        )

    has = (chain > 0, chain < 3)

    def sweep(c, s):
        now = s % 2
        later = 1 - now
        for piece in range(PIECES):
            for upper in range(2):
                @pl.when(has[upper])
                def _():
                    wait_bytes(
                        field.at[now, c, 0, piece_rows(piece)], edge_recv.at[c, now, upper, piece]
                    )

                relax_plane(c, now, later, CORE_PLANES if upper else 1, piece)

                @pl.when(has[upper] & (s < SWEEPS - 1))
                def _():
                    edge_copy(c, later, upper, piece).start()

        @pl.loop(2, CORE_PLANES)
        def _(p):
            relax_plane(c, now, later, p)

        for upper in range(2):
            @pl.when(has[upper])
            def _():
                for piece in range(PIECES):
                    edge_copy(c, now, upper, piece).wait_send()

    def begin_sweeps(c):
        wait_bytes(field.at[0, c, pl.ds(1, CORE_PLANES)], in_recv.at[c])
        for upper in range(2):
            @pl.when(has[upper])
            def _():
                for piece in range(PIECES):
                    edge_copy(c, 0, upper, piece).start()

    def sweeps(count, *parts):
        @pl.loop(0, count)
        def _(s):
            for c, first_sweep in parts:
                sweep(c, first_sweep + s)

    def out_sends(action, c):
        own_rows = pl.ds(pl.multiple_of(8 * (row_block % 2), 8), CORE_ROWS)
        dst = disp.at[
            own_inst, c, :, pl.ds(pl.multiple_of(CORE_ROWS * (row_block % 2), 8), CORE_ROWS), :
        ]
        for shift in range(4):
            to = (rank + shift) % 4
            action(
                field.at[0, c, pl.ds(1 + 2 * to, 2), own_rows, :], dst,
                out_send.at[c], out_recv.at[c], half * GROUP + 4 * core + to,
            )

    def start_out(c):
        out_sends(start_either, c)

    def share(of):
        return pl.ds(pl.multiple_of(SHARE * of, 8), SHARE)

    def inst_sends(source, own, dst, send, recv):
        for offset in INST_ORDER:
            to = inst_partner(inst, offset)
            remote(source(to), dst, send, recv, (to, slab)).start()
        pltpu.make_async_copy(own, dst, recv).start()

    def start_vin(c):
        wait_bytes(disp.at[:, c], out_recv.at[c])
        for p in range(2):
            inst_sends(
                lambda to: disp.at[:, c, p, share(to), :], disp.at[:, c, p, share(inst), :],
                vel_in.at[pl.ds(2 * inst, 2), c, p], vin_send.at[c, p], vin_recv.at[c, p],
            )

    def start_vout(c):
        for p in range(2):
            wait_bytes(vel_in.at[:, c, p], vin_recv.at[c, p])

            @pl.loop(0, 2)
            def _(i):
                rows = pl.ds(pl.multiple_of(8 * i, 8), 8)
                for lane in range(0, LANES, 128):
                    lanes = slice(lane, lane + 128)
                    u = [vel_in[n, c, p, rows, lanes] for n in range(INSTANCES)]
                    for n in range(INSTANCES):
                        total = None
                        for d in range(1, 8):
                            term = rate_factor(d) * (
                                u[(n - d) % INSTANCES] - u[(n + d) % INSTANCES]
                            )
                            total = term if total is None else total + term
                        rate[n, c, p, rows, lanes] = total

            inst_sends(
                lambda to: rate.at[pl.ds(2 * to, 2), c, p], rate.at[pl.ds(2 * inst, 2), c, p],
                vel_out.at[:, c, p, share(inst), :], vout_send.at[c, p], vout_recv.at[c, p],
            )

    wait_bytes(coef.at[:, :, pl.ds(0, DIRECT)], coef_recv)
    wait_bytes(coef.at[pl.ds(0, 3), :, shared], share_recv)
    begin_sweeps(0)
    start_in(1)
    sweeps(4, (0, 0))
    begin_sweeps(1)
    start_in(2)
    sweeps(4, (0, 4), (1, 0))
    start_out(0)
    begin_sweeps(2)
    sweeps(2, (1, 4), (2, 0))
    start_vin(0)
    sweeps(2, (1, 6), (2, 2))
    start_out(1)
    sweeps(4, (2, 4))
    start_out(2)
    start_vin(1)
    start_vout(0)
    start_vin(2)
    start_vout(1)
    start_vout(2)

    for c in range(3):
        in_sends(finish_either, c)
        out_sends(finish_either, c)
        for p in range(2):
            wait_bytes(vel_out.at[:, c, p], vout_recv.at[c, p])
            wait_bytes(vel_in.at[pl.ds(0, 14), c, p], vin_send.at[c, p])
            wait_bytes(rate.at[pl.ds(0, 14), c, p], vout_send.at[c, p])
    wait_bytes(coef.at[pl.ds(0, 3), :, shared], share_send)
    coef_sends(finish_either)
    part_sends(finish_either)
    table_sends(finish_either)
    code_sends(finish_either)


def per_device(prior_disp, surface_disp, springs, wall_row, wall_mask):
    surface = surface_disp.reshape(2, 3, 8, 128)
    code = jnp.where(wall_mask != 0, wall_row, -1).reshape(8, 128)
    f32 = jnp.float32
    dma = pltpu.SemaphoreType.DMA
    shape = jax.ShapeDtypeStruct(prior_disp.shape, f32)
    return pl.pallas_call(
        kernel,
        out_shape=(shape, shape),
        in_specs=[
            pl.BlockSpec(memory_space=pl.ANY),
            pl.BlockSpec(memory_space=pl.ANY),
            pl.BlockSpec(memory_space=pltpu.VMEM),
            pl.BlockSpec(memory_space=pl.ANY),
        ],
        out_specs=(pl.BlockSpec(memory_space=pltpu.VMEM),) * 2,
        scratch_shapes=[
            pltpu.VMEM((2, 3, CORE_PLANES + 2, ROWS, LANES), f32),
            pltpu.VMEM((4, CORE_PLANES // 2, ROWS, LANES), f32),
            pltpu.VMEM((4, 128, LANES), f32),
            pltpu.VMEM((INSTANCES, 3, 2, SHARE, LANES), f32),
            pltpu.VMEM((INSTANCES, 3, 2, SHARE, LANES), f32),
            pltpu.VMEM((3, 128, 128), f32),
            pltpu.VMEM((4, 8, 128), jnp.int32),
            pltpu.VMEM((3, CORE_PLANES, 8, LANES), f32),
            pltpu.VMEM((CORE_PLANES, 8, LANES), f32),
            dma((3,)), dma((3,)), dma, dma, dma, dma, dma, dma, dma, dma, dma, dma,
            dma((3, 2, 2, PIECES)), dma((3, 2, 2, PIECES)), dma((3,)), dma((3,)), dma((3, 2)), dma((3, 2)),
            dma((3, 2)), dma((3, 2)),
        ],
        compiler_params=pltpu.CompilerParams(
            collective_id=0, has_side_effects=True, vmem_limit_bytes=32 * 1024 * 1024
        ),
    )(prior_disp, surface, springs, code)


def solution(mesh):
    in_specs = (
        P("inst", None, "slab", None, None),
        P("inst", None, "slab"),
        P(None, "slab", None, None),
        P("slab", None),
        P("slab", None),
    )
    out_specs = (P("inst", None, "slab", None, None), P("inst", None, "slab", None, None))
    return jax.shard_map(
        per_device, mesh=mesh, in_specs=in_specs, out_specs=out_specs, check_vma=False
    )
```

```python
import math

import jax
import jax.numpy as jnp
from jax import lax
from jax.experimental import pallas as pl
from jax.experimental.pallas import tpu as pltpu
from jax.sharding import PartitionSpec as P

MESH = pl.DeviceIdType.MESH
SWEEPS = 8
ROWS = 72
CORE_PLANES = 8
INSTANCES = 16
GROUP = 8
INST_DEVICES = 8
CORE_ROWS = 64
PIECES = 3
PIECE_ROWS = 24
DIRECT = 16
SHARE = 16
LANES = 512


def rate_factor(d):
    return 2.0 * math.pi / INSTANCES * 0.5 * (-1.0) ** d / math.tan(math.pi * d / INSTANCES)


INST_ORDER = (1, 3, 4, 7, 2, 5, 6)


def window(row_block, first=0, count=ROWS):
    return pl.ds(pl.multiple_of(56 * (row_block % 2) + first, 8), count)


def inst_partner(inst, offset):
    return (inst // 4 + offset // 4) % 2 * 4 + (inst + offset) % 4


def kernel(
    prior, surface, springs, code,
    disp, vel_out,
    field, coef, own_coef, vel_in, rate, table, codes, wall, free,
    in_send, in_recv, coef_send, coef_recv, part_send, part_recv, share_send, share_recv, table_send, table_recv, code_send, code_recv,
    edge_send, edge_recv, out_send, out_recv, vin_send, vin_recv, vout_send, vout_recv,
):
    inst = lax.axis_index("inst")
    slab = lax.axis_index("slab")
    half = slab // GROUP
    rank = slab % GROUP
    row_block = rank // 2
    core = rank % 2
    own_inst = row_block // 2
    chain = 2 * half + core

    barrier = pltpu.get_barrier_semaphore()
    for shift in range(1, 2 * GROUP):
        pl.semaphore_signal(
            barrier, inc=1, device_id=(inst, (slab + shift) % (2 * GROUP)), device_id_type=MESH
        )
    for shift in range(1, INST_DEVICES):
        pl.semaphore_signal(
            barrier, inc=1, device_id=((inst + shift) % INST_DEVICES, slab), device_id_type=MESH
        )
    pl.semaphore_wait(barrier, 2 * GROUP - 1 + INST_DEVICES - 1)

    def remote(src, dst, send, recv, device):
        return pltpu.make_async_remote_copy(
            src_ref=src, dst_ref=dst, send_sem=send, recv_sem=recv,
            device_id=device, device_id_type=MESH,
        )

    def wait_bytes(ref, sem):
        pltpu.make_async_copy(ref, ref, sem).wait()

    def table_sends(action):
        for n in range(2):
            for k in range(4):
                target = k // 2 * GROUP + 4 * n + k % 2
                action(surface.at[n], table.at[:, pl.ds(pl.multiple_of(slab * 8, 8), 8), :],
                       table_send, table_recv, target)

    def code_sends(action):
        for n in range(2):
            action(code, codes.at[rank % 4], code_send, code_recv,
                   half * GROUP + 4 * n + row_block // 2)

    def start_either(src, dst, send, recv, target):
        @pl.when(target != slab)
        def _():
            remote(src, dst, send, recv, (inst, target)).start()

        @pl.when(target == slab)
        def _():
            pltpu.make_async_copy(src, dst, recv).start()

    def finish_either(src, dst, send, recv, target):
        @pl.when(target != slab)
        def _():
            remote(src, dst, send, recv, (inst, target)).wait_send()

    def row_sends(action, source, dst, send, recv):
        for shift in (0, 1, 3, 2):
            to = (row_block + shift) % 4
            action(source(to), dst, send, recv, half * GROUP + 2 * to + row_block // 2)

    def in_sends(action, c):
        row_sends(action, lambda to: prior.at[to // 2, c, :, window(to), :],
                  field.at[0, c, pl.ds(1 + 2 * (rank % 4), 2)], in_send.at[c], in_recv.at[c])

    quarter = inst % 4
    shared = pl.ds(DIRECT, ROWS - DIRECT)

    def coef_sends(action):
        row_sends(action, lambda to: own_coef.at[:, window(to, 0, DIRECT), :],
                  coef.at[:, rank % 4, pl.ds(0, DIRECT)], coef_send, coef_recv)

    def part_sends(action):
        row_sends(action, lambda to: own_coef.at[quarter, window(to, DIRECT, ROWS - DIRECT), :],
                  coef.at[quarter, rank % 4, shared], part_send, part_recv)

    def start_in(c):
        in_sends(start_either, c)

    @pl.loop(0, 32)
    def _(i):
        p = i // 16
        rows = pl.ds(pl.multiple_of(8 * (i % 16), 8), 8)
        s0 = springs[0, p, rows, :]
        s1 = springs[1, p, rows, :]
        s2 = springs[2, p, rows, :]
        scale = 0.45 / (s0 + s1 + s2)
        own_coef[p, rows, :] = s0 * scale
        own_coef[2 + p, rows, :] = s1 * scale

    part_sends(start_either)
    table_sends(start_either)
    code_sends(start_either)
    start_in(0)
    coef_sends(start_either)

    wait_bytes(coef.at[0, :, shared], part_recv)
    for offset in (1, 3, 2):
        mine = coef.at[quarter, :, shared]
        remote(
            mine, mine, share_send, share_recv, (inst // 4 * 4 + (inst + offset) % 4, slab)
        ).start()

    zero = jnp.zeros((8, LANES), jnp.float32)

    @pl.loop(0, 6)
    def _(i):
        for t in range(ROWS // 8):
            rows = slice(8 * t, 8 * t + 8)

            @pl.when(chain == 0)
            def _():
                field[i // 3, i % 3, 0, rows, :] = zero

            @pl.when(chain == 3)
            def _():
                field[i // 3, i % 3, CORE_PLANES + 1, rows, :] = zero

    @pl.loop(0, CORE_PLANES)
    def _(p):
        free[p] = zero
        for c in range(3):
            wall[c, p] = zero

    @pl.when(row_block % 2 == 0)
    def _():
        wait_bytes(table, table_recv)
        wait_bytes(codes, code_recv)
        low = [codes[s] & 127 for s in range(4)]
        high = [codes[s] >> 7 for s in range(4)]

        def pick(h, picked):
            hits = [high[s] == h for s in range(4)]
            result = []
            for c in range(3):
                row = jnp.broadcast_to(table[c, pl.ds(h, 1), :], (8, 128))
                for s in range(4):
                    value = jnp.take_along_axis(row, low[s], axis=1, mode="promise_in_bounds")
                    result.append(jnp.where(hits[s], value, picked[c * 4 + s]))
            return tuple(result)

        picked = lax.fori_loop(
            0, 128, pick, tuple(jnp.zeros((8, 128), jnp.float32) for _ in range(12))
        )
        for s in range(4):
            released = (codes[s] < 0).astype(jnp.float32)
            for row in range(8):
                lanes = slice(128 * (row % 4), 128 * (row % 4) + 128)
                free[2 * s + row // 4, 0:1, lanes] = released[row : row + 1, :]
                for c in range(3):
                    wall[c, 2 * s + row // 4, 0:1, lanes] = picked[c * 4 + s][row : row + 1, :]

    row_index = lax.broadcasted_iota(jnp.int32, (8, LANES), 0)
    first = row_index == 0
    last = row_index == 7

    def relax_plane(c, now, later, p, piece=None):
        tiles = ROWS // 8
        per = PIECE_ROWS // 8
        wanted = range(tiles) if piece is None else range(piece * per, piece * per + per)
        near = range(max(wanted[0] - 1, 0), min(wanted[-1] + 2, tiles))
        u = {t: field[now, c, p, 8 * t : 8 * t + 8, :] for t in near}
        down = {t: pltpu.roll(u[t], 1, 0) for t in near}
        up = {t: pltpu.roll(u[t], 7, 0) for t in near}
        if 0 in u:
            ghost = wall[c, p - 1, 0:1, :] + free[p - 1, 0:1, :] * u[0][0:1, :]
        for t in wanted:
            rows = slice(8 * t, 8 * t + 8)
            below = jnp.where(first, down[t - 1] if t else ghost, down[t])
            above = jnp.where(last, up[t + 1] if t + 1 < tiles else 0.0, up[t])
            beside = pltpu.roll(u[t], 1, 1) + pltpu.roll(u[t], LANES - 1, 1)
            planes = field[now, c, p - 1, rows, :] + field[now, c, p + 1, rows, :]
            field[later, c, p, rows, :] = (
                0.1 * u[t] + 0.45 * beside
                + coef[(p - 1) % 2, (p - 1) // 2, rows, :] * (planes - beside)
                + coef[2 + (p - 1) % 2, (p - 1) // 2, rows, :] * ((below + above) - beside)
            )

    def piece_rows(piece):
        return pl.ds(piece * PIECE_ROWS, PIECE_ROWS)

    def edge_copy(c, now, upper, piece):
        to = (chain + (1 if upper else 3)) % 4
        target = to // 2 * GROUP + 2 * row_block + to % 2
        src, dst = (CORE_PLANES, 0) if upper else (1, CORE_PLANES + 1)
        return remote(
            field.at[now, c, src, piece_rows(piece)], field.at[now, c, dst, piece_rows(piece)],
            edge_send.at[c, now, upper, piece], edge_recv.at[c, now, 1 - upper, piece],
            (inst, target),
        )

    has = (chain > 0, chain < 3)

    def sweep(c, s):
        now = s % 2
        later = 1 - now
        for piece in range(PIECES):
            for upper in range(2):
                @pl.when(has[upper])
                def _():
                    wait_bytes(
                        field.at[now, c, 0, piece_rows(piece)], edge_recv.at[c, now, upper, piece]
                    )

                relax_plane(c, now, later, CORE_PLANES if upper else 1, piece)

                @pl.when(has[upper] & (s < SWEEPS - 1))
                def _():
                    edge_copy(c, later, upper, piece).start()

        @pl.loop(2, CORE_PLANES)
        def _(p):
            relax_plane(c, now, later, p)

        for upper in range(2):
            @pl.when(has[upper])
            def _():
                for piece in range(PIECES):
                    edge_copy(c, now, upper, piece).wait_send()

    def begin_sweeps(c):
        wait_bytes(field.at[0, c, pl.ds(1, CORE_PLANES)], in_recv.at[c])
        for upper in range(2):
            @pl.when(has[upper])
            def _():
                for piece in range(PIECES):
                    edge_copy(c, 0, upper, piece).start()

    def sweeps(count, *parts):
        @pl.loop(0, count)
        def _(s):
            for c, first_sweep in parts:
                sweep(c, first_sweep + s)

    def out_sends(action, c):
        own_rows = pl.ds(pl.multiple_of(8 * (row_block % 2), 8), CORE_ROWS)
        dst = disp.at[
            own_inst, c, :, pl.ds(pl.multiple_of(CORE_ROWS * (row_block % 2), 8), CORE_ROWS), :
        ]
        for shift in range(4):
            to = (rank + shift) % 4
            action(
                field.at[0, c, pl.ds(1 + 2 * to, 2), own_rows, :], dst,
                out_send.at[c], out_recv.at[c], half * GROUP + 4 * core + to,
            )

    def start_out(c):
        out_sends(start_either, c)

    def share(of):
        return pl.ds(pl.multiple_of(SHARE * of, 8), SHARE)

    def inst_sends(source, own, dst, send, recv):
        for offset in INST_ORDER:
            to = inst_partner(inst, offset)
            remote(source(to), dst, send, recv, (to, slab)).start()
        pltpu.make_async_copy(own, dst, recv).start()

    def start_vin(c):
        wait_bytes(disp.at[:, c], out_recv.at[c])
        for p in range(2):
            inst_sends(
                lambda to: disp.at[:, c, p, share(to), :], disp.at[:, c, p, share(inst), :],
                vel_in.at[pl.ds(2 * inst, 2), c, p], vin_send.at[c, p], vin_recv.at[c, p],
            )

    def start_vout(c):
        for p in range(2):
            wait_bytes(vel_in.at[:, c, p], vin_recv.at[c, p])

            @pl.loop(0, 2)
            def _(i):
                rows = pl.ds(pl.multiple_of(8 * i, 8), 8)
                for lane in range(0, LANES, 128):
                    lanes = slice(lane, lane + 128)
                    u = [vel_in[n, c, p, rows, lanes] for n in range(INSTANCES)]
                    for n in range(INSTANCES):
                        total = None
                        for d in range(1, 8):
                            term = rate_factor(d) * (
                                u[(n - d) % INSTANCES] - u[(n + d) % INSTANCES]
                            )
                            total = term if total is None else total + term
                        rate[n, c, p, rows, lanes] = total

            inst_sends(
                lambda to: rate.at[pl.ds(2 * to, 2), c, p], rate.at[pl.ds(2 * inst, 2), c, p],
                vel_out.at[:, c, p, share(inst), :], vout_send.at[c, p], vout_recv.at[c, p],
            )

    wait_bytes(coef.at[:, :, pl.ds(0, DIRECT)], coef_recv)
    wait_bytes(coef.at[pl.ds(0, 3), :, shared], share_recv)
    begin_sweeps(0)
    start_in(1)
    sweeps(4, (0, 0))
    begin_sweeps(1)
    start_in(2)
    sweeps(4, (0, 4), (1, 0))
    start_out(0)
    begin_sweeps(2)
    sweeps(2, (1, 4), (2, 0))
    sweeps(2, (1, 6), (2, 2))
    start_out(1)
    start_vin(0)
    sweeps(4, (2, 4))
    start_out(2)
    start_vin(1)
    start_vout(0)
    start_vin(2)
    start_vout(1)
    start_vout(2)

    for c in range(3):
        in_sends(finish_either, c)
        out_sends(finish_either, c)
        for p in range(2):
            wait_bytes(vel_out.at[:, c, p], vout_recv.at[c, p])
            wait_bytes(vel_in.at[pl.ds(0, 14), c, p], vin_send.at[c, p])
            wait_bytes(rate.at[pl.ds(0, 14), c, p], vout_send.at[c, p])
    wait_bytes(coef.at[pl.ds(0, 3), :, shared], share_send)
    coef_sends(finish_either)
    part_sends(finish_either)
    table_sends(finish_either)
    code_sends(finish_either)


def per_device(prior_disp, surface_disp, springs, wall_row, wall_mask):
    surface = surface_disp.reshape(2, 3, 8, 128)
    code = jnp.where(wall_mask != 0, wall_row, -1).reshape(8, 128)
    f32 = jnp.float32
    dma = pltpu.SemaphoreType.DMA
    shape = jax.ShapeDtypeStruct(prior_disp.shape, f32)
    return pl.pallas_call(
        kernel,
        out_shape=(shape, shape),
        in_specs=[
            pl.BlockSpec(memory_space=pl.ANY),
            pl.BlockSpec(memory_space=pl.ANY),
            pl.BlockSpec(memory_space=pltpu.VMEM),
            pl.BlockSpec(memory_space=pl.ANY),
        ],
        out_specs=(pl.BlockSpec(memory_space=pltpu.VMEM),) * 2,
        scratch_shapes=[
            pltpu.VMEM((2, 3, CORE_PLANES + 2, ROWS, LANES), f32),
            pltpu.VMEM((4, CORE_PLANES // 2, ROWS, LANES), f32),
            pltpu.VMEM((4, 128, LANES), f32),
            pltpu.VMEM((INSTANCES, 3, 2, SHARE, LANES), f32),
            pltpu.VMEM((INSTANCES, 3, 2, SHARE, LANES), f32),
            pltpu.VMEM((3, 128, 128), f32),
            pltpu.VMEM((4, 8, 128), jnp.int32),
            pltpu.VMEM((3, CORE_PLANES, 8, LANES), f32),
            pltpu.VMEM((CORE_PLANES, 8, LANES), f32),
            dma((3,)), dma((3,)), dma, dma, dma, dma, dma, dma, dma, dma, dma, dma,
            dma((3, 2, 2, PIECES)), dma((3, 2, 2, PIECES)), dma((3,)), dma((3,)), dma((3, 2)), dma((3, 2)),
            dma((3, 2)), dma((3, 2)),
        ],
        compiler_params=pltpu.CompilerParams(
            collective_id=0, has_side_effects=True, vmem_limit_bytes=32 * 1024 * 1024
        ),
    )(prior_disp, surface, springs, code)


def solution(mesh):
    in_specs = (
        P("inst", None, "slab", None, None),
        P("inst", None, "slab"),
        P(None, "slab", None, None),
        P("slab", None),
        P("slab", None),
    )
    out_specs = (P("inst", None, "slab", None, None), P("inst", None, "slab", None, None))
    return jax.shard_map(
        per_device, mesh=mesh, in_specs=in_specs, out_specs=out_specs, check_vma=False
    )
```
